512 devices in a mesh: dp: 64 (over x, y, core), mp: 8 (over z).
Axes of the slice: x: 4, y: 8, z: 8, core: 2. Of those that a mesh axis runs over, the one named last changes fastest.
Arguments:
- tokens: bfloat16 [49152, 6144], P('dp', 'mp'), may hold values from -12 to 12, as said below
- cotangent: bfloat16 [49152, 512], P('dp'), may hold values from -12 to 12, as said below
- weights: float32 [6144, 512], P(('mp', 'dp')), may hold values from -0.078125 to 0.078125
- moment_one: float32 [6144, 512], P(('mp', 'dp')), may hold values from -3 to 3
- moment_two: float32 [6144, 512], P(('mp', 'dp')), may hold values from 0.05 to 2
Outputs:
- new_weights: float32 [6144, 512], P(('mp', 'dp'))
- new_moment_one: float32 [6144, 512], P(('mp', 'dp'))
- new_moment_two: float32 [6144, 512], P(('mp', 'dp'))
The draws below stay inside these ranges and needn't reach their ends.
Inputs may be any that keep to these rules, and one draw needn't show every extreme that they name: `tokens`: Real-valued activations. `cotangent`: Real-valued cotangents.
All inputs are finite; a program needn't handle non-finite values.
Results may differ from the reference program's by a relative error of at most 0.0045.
Values may be sent and summed in bfloat16 or wider, within the bound.
No kernel may reach another device: no remote copies, remote signals or barrier semaphores. Data moves between devices by JAX's collectives and lax.ppermute only.
A program may use at most 64 MiB of HBM per device.

```python
import math
import jax
import jax.numpy as jnp
from jax import lax

D = 6144
HEAD_DIM = 128
C = 512
TOKENS = 49152


def draw_tokens(key, part):
    key = jax.random.fold_in(key, 11)
    first_key, second_key = jax.random.split(key, 2)
    position = jnp.arange(D, dtype=jnp.float32) / D
    feature_scale = 0.3 * 10.0 ** (0.5 * jax.random.uniform(first_key, (D,), jnp.float32) + 0.5 * position)
    values = jnp.clip(jax.random.normal(second_key, (TOKENS, D), jnp.float32), -4.0, 4.0) * feature_scale
    return values.astype(jnp.bfloat16)


def draw_cotangent(key, part):
    key = jax.random.fold_in(key, 23)
    first_key, second_key = jax.random.split(key, 2)
    column_scale = 0.3 * 10.0 ** jax.random.uniform(first_key, (C,), jnp.float32)
    values = jnp.clip(jax.random.normal(second_key, (TOKENS, C), jnp.float32), -4.0, 4.0) * column_scale
    return values.astype(jnp.bfloat16)


def level_of(rng, extent, shards, low, high):
    gain = 1.0
    for dim, parts in shards:
        heights = jax.random.uniform(jax.random.fold_in(jax.random.fold_in(rng, 6), dim), (parts,), jnp.float32, low / len(shards), high / len(shards))
        gain = gain * jnp.repeat(jnp.exp(heights), extent[dim] // parts).reshape((-1,) + (1,) * (len(extent) - 1 - dim))
    return gain


def gaussian(stream_key, dims, deviation, most, shards=(), kind=jnp.bfloat16):
    entries = deviation * jax.random.normal(stream_key, dims, jnp.float32)
    if shards:
        entries = entries * level_of(stream_key, dims, shards, -0.22, 0.18)
    return jnp.clip(entries, -most, most).astype(kind)


def setup_inputs(seed: int = 0) -> dict:
    splits = jax.random.split(jax.random.key(seed), 6)
    tokens = draw_tokens(jax.random.fold_in(splits[5], 71), 0)
    cotangent = draw_cotangent(jax.random.fold_in(splits[5], 71), 0)
    weights = gaussian(splits[2], (D, C), D ** -0.5, 0.078125, ((0, 512),), jnp.float32)
    moment_one = gaussian(splits[3], (D, C), 0.5, 3.0, ((0, 512),), jnp.float32)
    moment_two = jnp.clip(jnp.exp(math.log(2.0) - 3.6888794 * jax.random.uniform(splits[4], (D, C), jnp.float32) ** level_of(splits[4], (D, C), ((0, 512),), -0.2, 0.2)), 0.05, 2.0)
    return dict(tokens=tokens, cotangent=cotangent, weights=weights, moment_one=moment_one, moment_two=moment_two)


radius = 8.0
rate = 0.005
decay_one = 0.9
decay_two = 0.95
weight_decay = 0.1
step_count = 10

def head_norm(values):
    shaped = values.reshape(values.shape[0], -1, HEAD_DIM)
    centred = shaped - lax.optimization_barrier(jnp.mean(shaped, axis=-1, keepdims=True))
    spread = lax.optimization_barrier(jnp.mean(centred * centred, axis=-1, keepdims=True))
    return (centred * lax.rsqrt(spread + 1e-06)).reshape(values.shape)

def head_grad(queries, cotangent):
    _, backward = jax.vjp(head_norm, queries)
    result, = backward(cotangent.astype(jnp.float32))
    return result.astype(jnp.bfloat16)

def gradient(tokens, cotangent, matrix, loss_scale):
    queries = jnp.dot(tokens, matrix.astype(jnp.bfloat16), preferred_element_type=jnp.float32)
    grads = head_grad(queries, cotangent)
    summed = lax.dot_general(tokens, grads, (((0,), (0,)), ((), ())), preferred_element_type=jnp.float32)
    return summed * loss_scale

def reference(tokens, cotangent, weights, moment_one, moment_two):
    loss_scale = 1.0 / math.sqrt(TOKENS)
    first = gradient(tokens, cotangent, weights, loss_scale)
    norm_value = jnp.sqrt(jnp.sum(first * first) + 1e-06)
    perturbed = weights + radius * first / norm_value
    second = gradient(tokens, cotangent, perturbed, loss_scale)
    new_moment_one = decay_one * moment_one + (1.0 - decay_one) * second
    new_moment_two = decay_two * moment_two + (1.0 - decay_two) * second * second
    correct_one = 1.0 - decay_one ** step_count
    correct_two = 1.0 - decay_two ** step_count
    update = new_moment_one / correct_one / (jnp.sqrt(new_moment_two / correct_two) + 1e-08)
    new_weights = weights - rate * (update + weight_decay * weights)
    return (new_weights, new_moment_one, new_moment_two)
```

```python
import math

import jax
import jax.numpy as jnp
from jax import lax
from jax.experimental import pallas as pl
from jax.experimental.pallas import tpu as pltpu
from jax.sharding import Mesh
from jax.sharding import PartitionSpec as P

HEAD_DIM = 128
CHUNKS = 1
PAD = 16
CORES = 2

radius = 8.0
rate = 0.005
decay_one = 0.9
decay_two = 0.95
weight_decay = 0.1
step_count = 10

BF16 = jnp.bfloat16
F32 = jnp.float32


def pieces_of(value, shape, row):
    high = value.astype(BF16).astype(F32)
    rest = value - high
    middle = rest.astype(BF16).astype(F32)
    low = rest - middle
    rows = lax.broadcasted_iota(jnp.int32, shape, len(shape) - 2)
    lanes = lax.broadcasted_iota(jnp.int32, shape, len(shape) - 1)
    picked = jnp.where(lanes == 0, high, jnp.where(lanes == 1, middle, jnp.where(lanes == 2, low, 0.0)))
    return jnp.where(rows == row, picked, 0.0)


def head_kernel(partial_ref, base_ref, scale_ref, cotangent_ref, queries_ref, out_ref):
    tokens = queries_ref.shape[0]
    width = queries_ref.shape[1]
    scale = scale_ref[0, 0]
    for head in range(width // HEAD_DIM):
        lanes = slice(head * HEAD_DIM, (head + 1) * HEAD_DIM)
        total = partial_ref[0, 0:tokens, lanes].astype(F32)
        for part in range(1, partial_ref.shape[0]):
            total = total + partial_ref[part, 0:tokens, lanes].astype(F32)
        queries = total * scale + base_ref[:, lanes]
        queries_ref[:, lanes] = queries
        cotangent = cotangent_ref[:, lanes].astype(F32)
        centred = queries - jnp.mean(queries, axis=-1, keepdims=True)
        spread = jnp.mean(centred * centred, axis=-1, keepdims=True)
        factor = lax.rsqrt(spread + 1e-06)
        normed = centred * factor
        level = jnp.mean(cotangent, axis=-1, keepdims=True)
        along = jnp.mean(cotangent * normed, axis=-1, keepdims=True)
        out_ref[:, lanes] = (factor * (cotangent - level - normed * along)).astype(BF16)


def head_step(partials, base, scale, cotangent):
    tokens, width = cotangent.shape
    vmem = pl.BlockSpec(memory_space=pltpu.VMEM)
    return pl.pallas_call(
        head_kernel,
        in_specs=[vmem, vmem, pl.BlockSpec(memory_space=pltpu.SMEM), vmem],
        out_specs=[vmem, vmem],
        out_shape=[
            jax.ShapeDtypeStruct((tokens, width), F32),
            jax.ShapeDtypeStruct((tokens, width), BF16),
        ],
        name="head_grad",
    )(partials, base, scale.reshape(1, 1), cotangent)


def local(tokens, cotangent, weights, moment_one, moment_two):
    count, depth = tokens.shape
    rows, columns = weights.shape
    groups = lax.axis_size("q")
    parts = lax.axis_size("mp")
    loss_scale = 1.0 / math.sqrt(count * groups * CORES)
    core = lax.axis_index("c")
    share = count // parts
    width = columns // CHUNKS
    half = groups * PAD

    feature = lax.broadcasted_iota(jnp.int32, (depth, CORES * half), 0)
    slot = lax.broadcasted_iota(jnp.int32, (depth, CORES * half), 1)
    owner = slot // half
    place = slot % half
    source = jnp.where(owner == 0, core, 1 - core)
    target = ((place // PAD) * CORES + source) * rows + place % PAD
    choose = ((feature == target) & (place % PAD < rows)).astype(BF16)
    spread_tokens = jnp.dot(tokens, choose, preferred_element_type=F32).astype(BF16)
    mine, other = spread_tokens[:, :half], spread_tokens[:, half:]

    cot = lax.dynamic_slice_in_dim(cotangent, lax.axis_index("mp") * share, share, 0)
    swap = [(0, 1), (1, 0)]

    def cut(array, chunk):
        return array[..., chunk * width : (chunk + 1) * width]

    def gather_rows(block):
        block = jnp.broadcast_to(block[None], (groups, PAD, width))
        own = lax.all_to_all(block, "q", 0, 0)
        return own, lax.ppermute(own, "c", swap)

    def queries_of(own, theirs):
        value = jnp.dot(mine, own.reshape(half, width), preferred_element_type=F32)
        value = value + jnp.dot(other, theirs.reshape(half, width), preferred_element_type=F32)
        return value.astype(BF16).reshape(parts, share, width)

    def gradient_of(grads):
        grads = lax.all_gather(grads, "mp", axis=0, tiled=True)

        def product(side):
            return lax.dot_general(side, grads, (((0,), (0,)), ((), ())), preferred_element_type=F32)

        theirs = lax.ppermute(product(other).astype(BF16), "c", swap)
        summed = (product(mine) + theirs.astype(F32)).astype(BF16)
        received = lax.all_to_all(summed.reshape(groups, PAD, width), "q", 0, 0)
        return jnp.sum(received.astype(F32), axis=0) * loss_scale

    one = jnp.ones((), F32)
    zeros = jnp.zeros((share, width), F32)
    padded = jnp.pad(weights.astype(BF16), ((0, PAD - rows), (0, 0)))
    gathered = [gather_rows(cut(padded, k)) for k in range(CHUNKS)]
    partials = [lax.all_to_all(queries_of(*pair), "mp", 0, 0) for pair in gathered]
    heads = [head_step(partials[k], zeros, one, cut(cot, k)) for k in range(CHUNKS)]
    queries = [pair[0] for pair in heads]
    firsts = [gradient_of(pair[1]) for pair in heads]

    exchanged = []
    squares = jnp.zeros((), F32)
    for first in firsts:
        block = first + pieces_of(jnp.sum(first * first), (PAD, width), rows)
        own, theirs = gather_rows(block.astype(BF16))
        total = jnp.sum(own[:, rows, :3].astype(F32)) + jnp.sum(theirs[:, rows, :3].astype(F32))
        tail = jnp.broadcast_to(pieces_of(total, (8, width), 0).astype(BF16), (parts, 8, width))
        sent = jnp.concatenate([queries_of(own, theirs), tail], axis=1)
        received = lax.all_to_all(sent, "mp", 0, 0)
        squares = squares + jnp.sum(received[:, share, :3].astype(F32))
        exchanged.append(received)
    scale = radius / jnp.sqrt(squares + 1e-06)
    seconds = [
        gradient_of(head_step(exchanged[k], queries[k], scale, cut(cot, k))[1]) for k in range(CHUNKS)
    ]
    second = jnp.concatenate(seconds, axis=1)[:rows]

    new_moment_one = decay_one * moment_one + (1.0 - decay_one) * second
    new_moment_two = decay_two * moment_two + (1.0 - decay_two) * second * second
    correct_one = 1.0 - decay_one**step_count
    correct_two = 1.0 - decay_two**step_count
    update = new_moment_one / correct_one / (jnp.sqrt(new_moment_two / correct_two) + 1e-08)
    new_weights = weights - rate * (update + weight_decay * weights)
    return (new_weights, new_moment_one, new_moment_two)


def solution(mesh):
    groups = mesh.shape["dp"] // CORES
    fine = Mesh(mesh.devices.reshape(groups, CORES, mesh.shape["mp"]), ("q", "c", "mp"))
    dp = ("q", "c")
    shard = P(("mp", "q", "c"), None)
    in_specs = (P(dp, "mp"), P(dp, None), shard, shard, shard)
    return jax.shard_map(local, mesh=fine, in_specs=in_specs, out_specs=(shard, shard, shard), check_vma=False)
```

```python
import functools
import math

import jax
import jax.numpy as jnp
from jax import lax
from jax.experimental import pallas as pl
from jax.experimental.pallas import tpu as pltpu
from jax.sharding import Mesh
from jax.sharding import PartitionSpec as P

HEAD_DIM = 128
PAD = 16
TAIL = 8
CORES = 2
MP = ("far", "near")
VMEM_BYTES = 16 * 1024 * 1024

radius = 8.0
rate = 0.005
decay_one = 0.9
decay_two = 0.95
weight_decay = 0.1
step_count = 10

BF16 = jnp.bfloat16
F32 = jnp.float32


def pieces_of(value, shape, row):
    high = value.astype(BF16).astype(F32)
    rest = value - high
    middle = rest.astype(BF16).astype(F32)
    low = rest - middle
    rows = lax.broadcasted_iota(jnp.int32, shape, len(shape) - 2)
    lanes = lax.broadcasted_iota(jnp.int32, shape, len(shape) - 1)
    picked = jnp.where(lanes == 0, high, jnp.where(lanes == 1, middle, jnp.where(lanes == 2, low, 0.0)))
    return jnp.where(rows == row, picked, 0.0)


def scalar_in(block, row):
    rows = lax.broadcasted_iota(jnp.int32, block.shape, len(block.shape) - 2)
    lanes = lax.broadcasted_iota(jnp.int32, block.shape, len(block.shape) - 1)
    return jnp.sum(jnp.where((rows == row) & (lanes < 3), block.astype(F32), 0.0))


def call(kernel, name, out_shape, *operands, cost=(0, 0)):
    vmem = pl.BlockSpec(memory_space=pltpu.VMEM)
    return pl.pallas_call(
        kernel,
        in_specs=[vmem] * len(operands),
        out_specs=jax.tree.map(lambda _: vmem, out_shape),
        out_shape=out_shape,
        compiler_params=pltpu.CompilerParams(vmem_limit_bytes=VMEM_BYTES),
        cost_estimate=pl.CostEstimate(flops=cost[0], bytes_accessed=cost[1], transcendentals=0),
        name=name,
    )(*operands)


def head_kernel(second, partial_ref, *refs):
    base_ref = refs[0] if second else None
    cotangent_ref = refs[1] if second else refs[0]
    out_ref = refs[-1]
    tokens, width = cotangent_ref.shape
    if second:
        squares = scalar_in(partial_ref[:, tokens : tokens + TAIL, 0:HEAD_DIM], 0)
        scale = radius * lax.rsqrt(jnp.full((1, HEAD_DIM), squares + 1e-06, F32))
    for head in range(width // HEAD_DIM):
        lanes = slice(head * HEAD_DIM, (head + 1) * HEAD_DIM)
        queries = partial_ref[0, 0:tokens, lanes].astype(F32)
        for part in range(1, partial_ref.shape[0]):
            queries = queries + partial_ref[part, 0:tokens, lanes].astype(F32)
        if second:
            queries = queries * scale + base_ref[:, lanes]
        else:
            refs[-2][:, lanes] = queries
        cotangent = cotangent_ref[:, lanes].astype(F32)
        centred = queries - jnp.mean(queries, axis=-1, keepdims=True)
        spread = jnp.mean(centred * centred, axis=-1, keepdims=True)
        factor = lax.rsqrt(spread + 1e-06)
        normed = centred * factor
        level = jnp.mean(cotangent, axis=-1, keepdims=True)
        along = jnp.mean(cotangent * normed, axis=-1, keepdims=True)
        out_ref[:, lanes] = (factor * (cotangent - level - normed * along)).astype(BF16)


def spread_kernel(weights_ref, out_ref):
    rows, width = weights_ref.shape
    out_ref[...] = jnp.zeros(out_ref.shape, BF16)
    block = weights_ref[...].astype(BF16)
    for part in range(out_ref.shape[0]):
        out_ref[part, 0:rows, :] = block


def pack_kernel(rows, loss_scale, received_ref, out_ref):
    total = received_ref[0].astype(F32)
    for part in range(1, received_ref.shape[0]):
        total = total + received_ref[part].astype(F32)
    total = total * loss_scale
    block = (total + pieces_of(jnp.sum(total * total), total.shape, rows)).astype(BF16)
    for part in range(out_ref.shape[0]):
        out_ref[part] = block


def change_kernel(rows, tokens_ref, own_ref, theirs_ref, value_ref, out_ref):
    parts, share, width = out_ref.shape
    share = share - TAIL
    squares = scalar_in(own_ref[:, :, 0:HEAD_DIM], rows) + scalar_in(theirs_ref[:, :, 0:HEAD_DIM], rows)
    tail = pieces_of(squares, (TAIL, width), 0).astype(BF16)
    first = theirs_ref[...].reshape(-1, width)
    step = parts // 2
    for side in range(2):
        picked = slice(side * step * share, (side + 1) * step * share)
        value = value_ref[picked, :] + jnp.dot(
            tokens_ref[picked, first.shape[0] :], first, preferred_element_type=F32
        )
        for part in range(step):
            out_ref[side * step + part, 0:share, :] = value[part * share : (part + 1) * share].astype(BF16)
            out_ref[side * step + part, share : share + TAIL, :] = tail


def local(tokens, cotangent, weights, moment_one, moment_two):
    count, depth = tokens.shape
    rows, columns = weights.shape
    groups = lax.axis_size("q")
    parts = lax.axis_size(MP)
    loss_scale = 1.0 / math.sqrt(count * groups * CORES)
    core = lax.axis_index("c")
    share = count // parts
    half = groups * PAD
    shape = jax.ShapeDtypeStruct

    feature = lax.broadcasted_iota(jnp.int32, (depth, CORES * half), 0)
    slot = lax.broadcasted_iota(jnp.int32, (depth, CORES * half), 1)
    place = slot % half
    source = jnp.where(slot < half, core, 1 - core)
    target = ((place // PAD) * CORES + source) * rows + place % PAD
    choose = ((feature == target) & (place % PAD < rows)).astype(BF16)
    spread_tokens = jnp.dot(tokens, choose, preferred_element_type=F32).astype(BF16)
    mine, other = spread_tokens[:, :half], spread_tokens[:, half:]

    cot = lax.dynamic_slice_in_dim(cotangent, lax.axis_index(MP) * share, share, 0)
    swap = [(0, 1), (1, 0)]

    def gather_rows(blocks):
        own = lax.all_to_all(blocks, "q", 0, 0)
        theirs = lax.ppermute(own, "c", swap)
        value = jnp.dot(mine, own.reshape(half, columns), preferred_element_type=F32)
        return own, theirs, value

    def gradient_of(grads):
        grads = lax.all_gather(grads, "near", axis=0, tiled=True)
        grads = lax.all_gather(grads, "far", axis=0, tiled=True)

        def product(side):
            return lax.dot_general(side, grads, (((0,), (0,)), ((), ())), preferred_element_type=F32)

        theirs = lax.ppermute(product(other).astype(BF16), "c", swap)
        summed = (product(mine) + theirs.astype(F32)).astype(BF16)
        return lax.all_to_all(summed.reshape(groups, PAD, columns), "q", 0, 0)

    blocks = shape((groups, PAD, columns), BF16)
    _, theirs, value = gather_rows(call(spread_kernel, "spread", blocks, weights))
    sent = value + jnp.dot(other, theirs.reshape(half, columns), preferred_element_type=F32)
    received = lax.all_to_all(sent.astype(BF16).reshape(parts, share, columns), MP, 0, 0)
    outs = (shape((share, columns), F32), shape((share, columns), BF16))
    queries, grads = call(functools.partial(head_kernel, False), "first_heads", outs, received, cot)
    received = gradient_of(grads)

    packed = call(functools.partial(pack_kernel, rows, loss_scale), "pack", blocks, received)
    own, theirs, value = gather_rows(packed)
    sent = call(
        functools.partial(change_kernel, rows),
        "change",
        shape((parts, share + TAIL, columns), BF16),
        spread_tokens,
        own,
        theirs,
        value,
        cost=(2 * count * half * columns, 8 * count * columns),
    )
    received = lax.all_to_all(sent, MP, 0, 0)
    grads = call(functools.partial(head_kernel, True), "second_heads", outs[1], received, queries, cot)
    received = gradient_of(grads)
    second = (jnp.sum(received.astype(F32), axis=0) * loss_scale)[:rows]

    new_moment_one = decay_one * moment_one + (1.0 - decay_one) * second
    new_moment_two = decay_two * moment_two + (1.0 - decay_two) * second * second
    correct_one = 1.0 - decay_one**step_count
    correct_two = 1.0 - decay_two**step_count
    update = new_moment_one / correct_one / (jnp.sqrt(new_moment_two / correct_two) + 1e-08)
    new_weights = weights - rate * (update + weight_decay * weights)
    return (new_weights, new_moment_one, new_moment_two)


def solution(mesh):
    groups = mesh.shape["dp"] // CORES
    far = mesh.shape["mp"] // 2
    fine = Mesh(mesh.devices.reshape(groups, CORES, far, 2), ("q", "c") + MP)
    dp = ("q", "c")
    shard = P(MP + dp, None)
    in_specs = (P(dp, MP), P(dp, None), shard, shard, shard)
    return jax.shard_map(local, mesh=fine, in_specs=in_specs, out_specs=(shard, shard, shard), check_vma=False)
```

```python
import functools
import math

import jax
import jax.numpy as jnp
from jax import lax
from jax.experimental import pallas as pl
from jax.experimental.pallas import tpu as pltpu
from jax.sharding import Mesh
from jax.sharding import PartitionSpec as P

HEAD_DIM = 128
TAIL = 8
CORES = 2
MP = ("far", "near")
VMEM_BYTES = 16 * 1024 * 1024

radius = 8.0
rate = 0.005
decay_one = 0.9
decay_two = 0.95
weight_decay = 0.1
step_count = 10

BF16 = jnp.bfloat16
F32 = jnp.float32


def pieces_of(value, shape, row):
    high = value.astype(BF16).astype(F32)
    rest = value - high
    middle = rest.astype(BF16).astype(F32)
    low = rest - middle
    rows = lax.broadcasted_iota(jnp.int32, shape, len(shape) - 2)
    lanes = lax.broadcasted_iota(jnp.int32, shape, len(shape) - 1)
    picked = jnp.where(lanes == 0, high, jnp.where(lanes == 1, middle, jnp.where(lanes == 2, low, 0.0)))
    return jnp.where(rows == row, picked, 0.0)


def scalar_in(block, row):
    rows = lax.broadcasted_iota(jnp.int32, block.shape, len(block.shape) - 2)
    lanes = lax.broadcasted_iota(jnp.int32, block.shape, len(block.shape) - 1)
    return jnp.sum(jnp.where((rows == row) & (lanes < 3), block.astype(F32), 0.0))


def call(kernel, name, out_shape, *operands, cost=(0, 0)):
    vmem = pl.BlockSpec(memory_space=pltpu.VMEM)
    smem = pl.BlockSpec(memory_space=pltpu.SMEM)
    return pl.pallas_call(
        kernel,
        in_specs=[smem if operand.dtype == jnp.int32 else vmem for operand in operands],
        out_specs=jax.tree.map(lambda _: vmem, out_shape),
        out_shape=out_shape,
        compiler_params=pltpu.CompilerParams(vmem_limit_bytes=VMEM_BYTES),
        cost_estimate=pl.CostEstimate(flops=cost[0], bytes_accessed=cost[1], transcendentals=0),
        name=name,
    )(*operands)


def head_kernel(second, partial_ref, *refs):
    base_ref = refs[0] if second else None
    cotangent_ref = refs[1] if second else refs[0]
    out_ref = refs[-1]
    tokens, width = cotangent_ref.shape
    if second:
        squares = scalar_in(partial_ref[:, tokens : tokens + TAIL, 0:HEAD_DIM], 0)
        scale = radius * lax.rsqrt(jnp.full((1, HEAD_DIM), squares + 1e-06, F32))
    for head in range(width // HEAD_DIM):
        lanes = slice(head * HEAD_DIM, (head + 1) * HEAD_DIM)
        queries = partial_ref[0, 0:tokens, lanes].astype(F32)
        for part in range(1, partial_ref.shape[0]):
            queries = queries + partial_ref[part, 0:tokens, lanes].astype(F32)
        if second:
            queries = queries * scale + base_ref[:, lanes]
        else:
            refs[-2][:, lanes] = queries
        cotangent = cotangent_ref[:, lanes].astype(F32)
        centred = queries - jnp.mean(queries, axis=-1, keepdims=True)
        spread = jnp.mean(centred * centred, axis=-1, keepdims=True)
        factor = lax.rsqrt(spread + 1e-06)
        normed = centred * factor
        level = jnp.mean(cotangent, axis=-1, keepdims=True)
        along = jnp.mean(cotangent * normed, axis=-1, keepdims=True)
        out_ref[:, lanes] = (factor * (cotangent - level - normed * along)).astype(BF16)


def swapped(core, one, two):
    return jnp.where(core == 0, one, two), jnp.where(core == 0, two, one)


def spread_kernel(core_ref, weights_ref, theirs_ref, out_ref):
    width = theirs_ref.shape[1]
    mine = swapped(core_ref[0, 0], weights_ref[:, :width], weights_ref[:, width:])[0]
    pair = swapped(core_ref[0, 0], mine, theirs_ref[...].astype(F32))
    block = jnp.concatenate(pair, axis=0).astype(BF16)
    for part in range(out_ref.shape[0]):
        out_ref[part] = block


def pack_kernel(loss_scale, received_ref, out_ref):
    total = received_ref[0].astype(F32)
    for part in range(1, received_ref.shape[0]):
        total = total + received_ref[part].astype(F32)
    block = (total * loss_scale).astype(BF16)
    for part in range(out_ref.shape[0]):
        out_ref[part] = block


def fold_kernel(loss_scale, core_ref, received_ref, kept_ref, given_ref):
    total = received_ref[0].astype(F32)
    for part in range(1, received_ref.shape[0]):
        total = total + received_ref[part].astype(F32)
    total = total * loss_scale
    rows = kept_ref.shape[0]
    kept_ref[...], given_ref[...] = swapped(core_ref[0, 0], total[:rows], total[rows:])


def update_kernel(core_ref, mine_ref, theirs_ref, weights_ref, one_ref, two_ref, *out_refs):
    width = mine_ref.shape[1]
    correct_one = 1.0 - decay_one**step_count
    correct_two = 1.0 - decay_two**step_count
    for side, second in enumerate(swapped(core_ref[0, 0], mine_ref[...], theirs_ref[...])):
        lanes = slice(side * width, (side + 1) * width)
        weights = weights_ref[:, lanes]
        new_one = decay_one * one_ref[:, lanes] + (1.0 - decay_one) * second
        new_two = decay_two * two_ref[:, lanes] + (1.0 - decay_two) * second * second
        update = new_one / correct_one / (jnp.sqrt(new_two / correct_two) + 1e-08)
        out_refs[0][:, lanes] = weights - rate * (update + weight_decay * weights)
        out_refs[1][:, lanes] = new_one
        out_refs[2][:, lanes] = new_two


def change_kernel(tokens_ref, first_ref, squares_ref, other_ref, out_ref):
    parts, share, width = out_ref.shape
    share = share - TAIL
    tail = pieces_of(squares_ref[...] + other_ref[...], (TAIL, width), 0).astype(BF16)
    step = 2
    for group in range(parts // step):
        picked = slice(group * step * share, (group + 1) * step * share)
        value = jnp.dot(tokens_ref[picked, :], first_ref[...], preferred_element_type=F32)
        for part in range(step):
            out_ref[group * step + part, 0:share, :] = value[part * share : (part + 1) * share].astype(BF16)
            out_ref[group * step + part, share : share + TAIL, :] = tail


def local(tokens, cotangent, weights, moment_one, moment_two):
    count, depth = tokens.shape
    rows, columns = weights.shape
    groups = lax.axis_size("q")
    parts = lax.axis_size(MP)
    loss_scale = 1.0 / math.sqrt(count * groups * CORES)
    core = lax.axis_index("c")
    share = count // parts
    width = columns // CORES
    shape = jax.ShapeDtypeStruct
    swap = [(0, 1), (1, 0)]

    which = core.reshape(1, 1).astype(jnp.int32)
    given = lax.dynamic_slice_in_dim(weights, (1 - core) * width, width, 1).astype(BF16)
    theirs = lax.ppermute(given, "c", swap)
    blocks = shape((groups, CORES * rows, width), BF16)
    spread = call(spread_kernel, "spread", blocks, which, weights, theirs)
    spread, tokens = lax.optimization_barrier((spread, tokens))

    theirs = lax.ppermute(tokens, "c", swap)
    pair = [side.reshape(parts, share, depth) for side in (tokens, theirs)]
    tokens = jnp.concatenate(pair, axis=1).reshape(-1, depth)

    cot = lax.dynamic_slice_in_dim(cotangent, lax.axis_index(MP) * share, share, 0)
    kept = lax.dynamic_slice_in_dim(cot, core * width, width, 1)
    given = lax.dynamic_slice_in_dim(cot, (1 - core) * width, width, 1)
    cot = jnp.concatenate([kept, lax.ppermute(given, "c", swap)], axis=0)

    def exchange(blocks):
        return lax.all_to_all(blocks, "q", 0, 0)

    def gradient_of(grads):
        grads = lax.all_gather(grads, "near", axis=0, tiled=True)
        grads = lax.all_gather(grads, "far", axis=0, tiled=True)
        summed = lax.dot_general(tokens, grads, (((0,), (0,)), ((), ())), preferred_element_type=F32)
        return exchange(summed.astype(BF16).reshape(groups, CORES * rows, width))

    gathered = exchange(spread)
    sent = jnp.dot(tokens, gathered.reshape(depth, width), preferred_element_type=F32)
    received = lax.all_to_all(sent.astype(BF16).reshape(parts, CORES * share, width), MP, 0, 0)
    outs = (shape((CORES * share, width), F32), shape((CORES * share, width), BF16))
    queries, grads = call(functools.partial(head_kernel, False), "first_heads", outs, received, cot)
    received = gradient_of(grads)

    packed = call(functools.partial(pack_kernel, loss_scale), "pack", blocks, received)
    first = exchange(packed).reshape(depth, width)
    squares = jnp.sum(jnp.square(first.astype(F32))).reshape(1, 1)
    sent = call(
        change_kernel,
        "change",
        shape((parts, CORES * share + TAIL, width), BF16),
        tokens,
        first,
        squares,
        lax.ppermute(squares, "c", swap),
        cost=(2 * CORES * count * depth * width, 2 * CORES * count * depth),
    )
    received = lax.all_to_all(sent, MP, 0, 0)
    grads = call(functools.partial(head_kernel, True), "second_heads", outs[1], received, queries, cot)
    half = shape((rows, width), F32)
    received = gradient_of(grads)
    mine, given = call(functools.partial(fold_kernel, loss_scale), "fold", (half, half), which, received)
    theirs = lax.ppermute(given, "c", swap)
    whole = shape((rows, columns), F32)
    return call(
        update_kernel, "update", (whole,) * 3, which, mine, theirs, weights, moment_one, moment_two
    )


def solution(mesh):
    groups = mesh.shape["dp"] // CORES
    far = mesh.shape["mp"] // 2
    fine = Mesh(mesh.devices.reshape(groups, CORES, far, 2), ("q", "c") + MP)
    dp = ("q", "c")
    shard = P(MP + dp, None)
    in_specs = (P(dp, MP), P(dp, None), shard, shard, shard)
    return jax.shard_map(local, mesh=fine, in_specs=in_specs, out_specs=(shard,) * 3, check_vma=False)
```

```python
import functools
import math

import jax
import jax.numpy as jnp
from jax import lax
from jax.experimental import pallas as pl
from jax.experimental.pallas import tpu as pltpu
from jax.sharding import Mesh
from jax.sharding import PartitionSpec as P

HEAD_DIM = 128
TAIL = 8
CORES = 2
MP = ("far", "near")
VMEM_BYTES = 16 * 1024 * 1024

radius = 8.0
rate = 0.005
decay_one = 0.9
decay_two = 0.95
weight_decay = 0.1
step_count = 10

BF16 = jnp.bfloat16
F32 = jnp.float32


def pieces_of(value, shape, row):
    high = value.astype(BF16).astype(F32)
    rest = value - high
    middle = rest.astype(BF16).astype(F32)
    low = rest - middle
    rows = lax.broadcasted_iota(jnp.int32, shape, len(shape) - 2)
    lanes = lax.broadcasted_iota(jnp.int32, shape, len(shape) - 1)
    picked = jnp.where(lanes == 0, high, jnp.where(lanes == 1, middle, jnp.where(lanes == 2, low, 0.0)))
    return jnp.where(rows == row, picked, 0.0)


def call(kernel, name, out_shape, *operands, cost=(0, 0)):
    vmem = pl.BlockSpec(memory_space=pltpu.VMEM)
    smem = pl.BlockSpec(memory_space=pltpu.SMEM)
    return pl.pallas_call(
        kernel,
        in_specs=[smem if operand.dtype == jnp.int32 else vmem for operand in operands],
        out_specs=jax.tree.map(lambda _: vmem, out_shape),
        out_shape=out_shape,
        compiler_params=pltpu.CompilerParams(vmem_limit_bytes=VMEM_BYTES),
        cost_estimate=pl.CostEstimate(flops=cost[0], bytes_accessed=cost[1], transcendentals=0),
        name=name,
    )(*operands)


def head_kernel(second, partial_ref, *refs):
    squares_ref, base_ref = refs[:2] if second else (None, None)
    cotangent_ref = refs[2] if second else refs[0]
    out_ref = refs[-1]
    tokens, width = cotangent_ref.shape
    if second:
        squares = squares_ref[0:1, :] + squares_ref[TAIL : TAIL + 1, :]
        scale = radius * lax.rsqrt(squares + 1e-06)
    for head in range(width // HEAD_DIM):
        lanes = slice(head * HEAD_DIM, (head + 1) * HEAD_DIM)
        queries = partial_ref[0, 0:tokens, lanes].astype(F32)
        for part in range(1, partial_ref.shape[0]):
            queries = queries + partial_ref[part, 0:tokens, lanes].astype(F32)
        if second:
            queries = queries * scale + base_ref[:, lanes]
        else:
            refs[-2][:, lanes] = queries
        cotangent = cotangent_ref[:, lanes].astype(F32)
        centred = queries - jnp.mean(queries, axis=-1, keepdims=True)
        spread = jnp.mean(centred * centred, axis=-1, keepdims=True)
        factor = lax.rsqrt(spread + 1e-06)
        normed = centred * factor
        level = jnp.mean(cotangent, axis=-1, keepdims=True)
        along = jnp.mean(cotangent * normed, axis=-1, keepdims=True)
        out_ref[:, lanes] = (factor * (cotangent - level - normed * along)).astype(BF16)


def swapped(core, one, two):
    return jnp.where(core == 0, one, two), jnp.where(core == 0, two, one)


def spread_kernel(core_ref, weights_ref, out_ref):
    width = out_ref.shape[2]
    pair = []
    for side in range(CORES):
        pair.append(swapped(core_ref[0, 0], weights_ref[side, :, :width], weights_ref[side, :, width:])[0])
    block = jnp.concatenate(pair, axis=0).astype(BF16)
    for part in range(out_ref.shape[0]):
        out_ref[part] = block


def pack_kernel(loss_scale, received_ref, out_ref):
    total = received_ref[0].astype(F32)
    for part in range(1, received_ref.shape[0]):
        total = total + received_ref[part].astype(F32)
    block = (total * loss_scale).astype(BF16)
    for part in range(out_ref.shape[0]):
        out_ref[part] = block


def fold_kernel(loss_scale, received_ref, out_ref):
    total = received_ref[0].astype(F32)
    for part in range(1, received_ref.shape[0]):
        total = total + received_ref[part].astype(F32)
    out_ref[...] = total * loss_scale


def update_kernel(core_ref, second_ref, weights_ref, one_ref, two_ref, *out_refs):
    rows = weights_ref.shape[0]
    width = second_ref.shape[1]
    correct_one = 1.0 - decay_one**step_count
    correct_two = 1.0 - decay_two**step_count
    for side in range(CORES):
        start = side * CORES * rows
        lanes = slice(side * width, (side + 1) * width)
        second = swapped(
            core_ref[0, 0],
            second_ref[start : start + rows, :],
            second_ref[start + rows : start + CORES * rows, :],
        )[0]
        weights = weights_ref[:, lanes]
        new_one = decay_one * one_ref[:, lanes] + (1.0 - decay_one) * second
        new_two = decay_two * two_ref[:, lanes] + (1.0 - decay_two) * second * second
        update = new_one / correct_one / (jnp.sqrt(new_two / correct_two) + 1e-08)
        out_refs[0][:, lanes] = weights - rate * (update + weight_decay * weights)
        out_refs[1][:, lanes] = new_one
        out_refs[2][:, lanes] = new_two


def total_kernel(received_ref, out_ref):
    parts, share, _ = received_ref.shape
    block = received_ref[0, share - TAIL : share, 0:HEAD_DIM].astype(F32)
    for part in range(1, parts):
        block = block + received_ref[part, share - TAIL : share, 0:HEAD_DIM].astype(F32)
    out_ref[...] = jnp.full(out_ref.shape, jnp.sum(block), F32)


def queries_kernel(second, tokens_ref, first_ref, out_ref):
    parts, share, width = out_ref.shape
    if second:
        share = share - TAIL
        first = first_ref[...].astype(F32)
        tail = pieces_of(jnp.sum(first * first), (TAIL, width), 0).astype(BF16)
    step = 2
    for group in range(parts // step):
        picked = slice(group * step * share, (group + 1) * step * share)
        value = jnp.dot(tokens_ref[picked, :], first_ref[...], preferred_element_type=F32)
        for part in range(step):
            out_ref[group * step + part, 0:share, :] = value[part * share : (part + 1) * share].astype(BF16)
            if second:
                out_ref[group * step + part, share : share + TAIL, :] = tail


def local(tokens, cotangent, weights, moment_one, moment_two):
    count, depth = tokens.shape
    rows, columns = weights.shape
    groups = lax.axis_size("q")
    parts = lax.axis_size(MP)
    loss_scale = 1.0 / math.sqrt(count * groups * CORES)
    core = lax.axis_index("c")
    share = count // parts
    width = columns // CORES
    shape = jax.ShapeDtypeStruct
    swap = [(0, 1), (1, 0)]

    which = core.reshape(1, 1).astype(jnp.int32)
    blocks = shape((groups, CORES * rows, width), BF16)
    spread = call(spread_kernel, "spread", blocks, which, lax.all_gather(weights, "c", axis=0))
    spread, tokens = lax.optimization_barrier((spread, tokens))

    theirs = lax.ppermute(tokens, "c", swap)
    pair = [side.reshape(parts, share, depth) for side in (tokens, theirs)]
    tokens = jnp.concatenate(pair, axis=1).reshape(-1, depth)

    cot = lax.dynamic_slice_in_dim(cotangent, lax.axis_index(MP) * share, share, 0)
    kept = lax.dynamic_slice_in_dim(cot, core * width, width, 1)
    given = lax.dynamic_slice_in_dim(cot, (1 - core) * width, width, 1)
    cot = jnp.concatenate([kept, lax.ppermute(given, "c", swap)], axis=0)

    def exchange(blocks):
        return lax.all_to_all(blocks, "q", 0, 0)

    def queries_of(second, blocks):
        return call(
            functools.partial(queries_kernel, second),
            "second_queries" if second else "first_queries",
            shape((parts, CORES * share + TAIL * second, width), BF16),
            tokens,
            exchange(blocks).reshape(depth, width),
            cost=(2 * CORES * count * depth * width, 2 * CORES * count * depth),
        )

    def gradient_of(grads):
        grads = lax.all_gather(grads, "near", axis=0, tiled=True)
        grads = lax.all_gather(grads, "far", axis=0, tiled=True)
        summed = lax.dot_general(tokens, grads, (((0,), (0,)), ((), ())), preferred_element_type=F32)
        return exchange(summed.astype(BF16).reshape(groups, CORES * rows, width))

    sent = queries_of(False, spread)
    received = lax.all_to_all(sent, MP, 0, 0)
    outs = (shape((CORES * share, width), F32), shape((CORES * share, width), BF16))
    queries, grads = call(functools.partial(head_kernel, False), "first_heads", outs, received, cot)
    received = gradient_of(grads)

    packed = call(functools.partial(pack_kernel, loss_scale), "pack", blocks, received)
    sent = queries_of(True, packed)
    received = lax.all_to_all(sent, MP, 0, 0)
    squares = call(total_kernel, "total", shape((TAIL, HEAD_DIM), F32), received)
    squares = lax.all_gather(squares, "c", axis=0, tiled=True)
    grads = call(
        functools.partial(head_kernel, True), "second_heads", outs[1], received, squares, queries, cot
    )
    second = call(
        functools.partial(fold_kernel, loss_scale),
        "fold",
        shape((CORES * rows, width), F32),
        gradient_of(grads),
    )
    second = lax.all_gather(second, "c", axis=0, tiled=True)
    whole = shape((rows, columns), F32)
    return call(update_kernel, "update", (whole,) * 3, which, second, weights, moment_one, moment_two)


def solution(mesh):
    groups = mesh.shape["dp"] // CORES
    far = mesh.shape["mp"] // 2
    fine = Mesh(mesh.devices.reshape(groups, CORES, far, 2), ("q", "c") + MP)
    dp = ("q", "c")
    shard = P(MP + dp, None)
    in_specs = (P(dp, MP), P(dp, None), shard, shard, shard)
    return jax.shard_map(local, mesh=fine, in_specs=in_specs, out_specs=(shard,) * 3, check_vma=False)
```

```python
import functools
import math

import jax
import jax.numpy as jnp
from jax import lax
from jax.experimental import pallas as pl
from jax.experimental.pallas import tpu as pltpu
from jax.sharding import Mesh
from jax.sharding import PartitionSpec as P

HEAD_DIM = 128
TAIL = 8
CORES = 2
MP = ("far", "near")
VMEM_BYTES = 16 * 1024 * 1024

radius = 8.0
rate = 0.005
decay_one = 0.9
decay_two = 0.95
weight_decay = 0.1
step_count = 10

BF16 = jnp.bfloat16
F32 = jnp.float32


def pieces_of(value, shape, row):
    high = value.astype(BF16).astype(F32)
    rest = value - high
    middle = rest.astype(BF16).astype(F32)
    low = rest - middle
    rows = lax.broadcasted_iota(jnp.int32, shape, len(shape) - 2)
    lanes = lax.broadcasted_iota(jnp.int32, shape, len(shape) - 1)
    picked = jnp.where(lanes == 0, high, jnp.where(lanes == 1, middle, jnp.where(lanes == 2, low, 0.0)))
    return jnp.where(rows == row, picked, 0.0)


def call(kernel, name, out_shape, *operands, cost=(0, 0)):
    vmem = pl.BlockSpec(memory_space=pltpu.VMEM)
    smem = pl.BlockSpec(memory_space=pltpu.SMEM)
    return pl.pallas_call(
        kernel,
        in_specs=[smem if operand.dtype == jnp.int32 else vmem for operand in operands],
        out_specs=jax.tree.map(lambda _: vmem, out_shape),
        out_shape=out_shape,
        compiler_params=pltpu.CompilerParams(vmem_limit_bytes=VMEM_BYTES),
        cost_estimate=pl.CostEstimate(flops=cost[0], bytes_accessed=cost[1], transcendentals=0),
        name=name,
    )(*operands)


def head_kernel(second, partial_ref, *refs):
    squares_ref, base_ref = refs[:2] if second else (None, None)
    cotangent_ref = refs[2] if second else refs[0]
    out_ref = refs[-1]
    tokens, width = cotangent_ref.shape
    if second:
        squares = squares_ref[0:1, :] + squares_ref[TAIL : TAIL + 1, :]
        scale = radius * lax.rsqrt(squares + 1e-06)
    for head in range(width // HEAD_DIM):
        lanes = slice(head * HEAD_DIM, (head + 1) * HEAD_DIM)
        queries = partial_ref[0, 0:tokens, lanes].astype(F32)
        for part in range(1, partial_ref.shape[0]):
            queries = queries + partial_ref[part, 0:tokens, lanes].astype(F32)
        if second:
            queries = queries * scale + base_ref[:, lanes]
        else:
            refs[-2][:, lanes] = queries
        cotangent = cotangent_ref[:, lanes].astype(F32)
        centred = queries - jnp.mean(queries, axis=-1, keepdims=True)
        spread = jnp.mean(centred * centred, axis=-1, keepdims=True)
        factor = lax.rsqrt(spread + 1e-06)
        normed = centred * factor
        level = jnp.mean(cotangent, axis=-1, keepdims=True)
        along = jnp.mean(cotangent * normed, axis=-1, keepdims=True)
        out_ref[:, lanes] = (factor * (cotangent - level - normed * along)).astype(BF16)


def swapped(core, one, two):
    return jnp.where(core == 0, one, two), jnp.where(core == 0, two, one)


def spread_kernel(core_ref, weights_ref, out_ref):
    width = out_ref.shape[2]
    pair = []
    for side in range(CORES):
        pair.append(swapped(core_ref[0, 0], weights_ref[side, :, :width], weights_ref[side, :, width:])[0])
    block = jnp.concatenate(pair, axis=0).astype(BF16)
    for part in range(out_ref.shape[0]):
        out_ref[part] = block


def pack_kernel(loss_scale, received_ref, out_ref):
    total = received_ref[0].astype(F32)
    for part in range(1, received_ref.shape[0]):
        total = total + received_ref[part].astype(F32)
    block = (total * loss_scale).astype(BF16)
    for part in range(out_ref.shape[0]):
        out_ref[part] = block


def fold_kernel(loss_scale, received_ref, out_ref):
    total = received_ref[0].astype(F32)
    for part in range(1, received_ref.shape[0]):
        total = total + received_ref[part].astype(F32)
    out_ref[...] = total * loss_scale


def update_kernel(core_ref, second_ref, weights_ref, one_ref, two_ref, *out_refs):
    rows = weights_ref.shape[0]
    width = second_ref.shape[1]
    correct_one = 1.0 - decay_one**step_count
    correct_two = 1.0 - decay_two**step_count
    for side in range(CORES):
        start = side * CORES * rows
        lanes = slice(side * width, (side + 1) * width)
        second = swapped(
            core_ref[0, 0],
            second_ref[start : start + rows, :],
            second_ref[start + rows : start + CORES * rows, :],
        )[0]
        weights = weights_ref[:, lanes]
        new_one = decay_one * one_ref[:, lanes] + (1.0 - decay_one) * second
        new_two = decay_two * two_ref[:, lanes] + (1.0 - decay_two) * second * second
        update = new_one / correct_one / (jnp.sqrt(new_two / correct_two) + 1e-08)
        out_refs[0][:, lanes] = weights - rate * (update + weight_decay * weights)
        out_refs[1][:, lanes] = new_one
        out_refs[2][:, lanes] = new_two


def total_kernel(received_ref, out_ref):
    parts, share, _ = received_ref.shape
    block = received_ref[0, share - TAIL : share, 0:HEAD_DIM].astype(F32)
    for part in range(1, parts):
        block = block + received_ref[part, share - TAIL : share, 0:HEAD_DIM].astype(F32)
    out_ref[...] = jnp.full(out_ref.shape, jnp.sum(block), F32)


def queries_kernel(second, tokens_ref, first_ref, out_ref):
    parts, share, width = out_ref.shape
    if second:
        share = share - TAIL
        first = first_ref[...].astype(F32)
        tail = pieces_of(jnp.sum(first * first), (TAIL, width), 0).astype(BF16)
    step = 2
    for group in range(parts // step):
        picked = slice(group * step * share, (group + 1) * step * share)
        value = jnp.dot(tokens_ref[picked, :], first_ref[...], preferred_element_type=F32)
        for part in range(step):
            out_ref[group * step + part, 0:share, :] = value[part * share : (part + 1) * share].astype(BF16)
            if second:
                out_ref[group * step + part, share : share + TAIL, :] = tail


def local(tokens, cotangent, weights, moment_one, moment_two):
    count, depth = tokens.shape
    rows, columns = weights.shape
    groups = lax.axis_size("q")
    parts = lax.axis_size(MP)
    loss_scale = 1.0 / math.sqrt(count * groups * CORES)
    core = lax.axis_index("c")
    share = count // parts
    width = columns // CORES
    shape = jax.ShapeDtypeStruct
    swap = [(0, 1), (1, 0)]

    which = core.reshape(1, 1).astype(jnp.int32)
    blocks = shape((groups, CORES * rows, width), BF16)
    spread = call(spread_kernel, "spread", blocks, which, lax.all_gather(weights, "c", axis=0))
    spread, tokens = lax.optimization_barrier((spread, tokens))

    theirs = lax.ppermute(tokens, "c", swap)
    pair = [side.reshape(parts, share, depth) for side in (tokens, theirs)]
    tokens = jnp.concatenate(pair, axis=1).reshape(-1, depth)

    cot = lax.dynamic_slice_in_dim(cotangent, lax.axis_index(MP) * share, share, 0)
    kept = lax.dynamic_slice_in_dim(cot, core * width, width, 1)
    given = lax.dynamic_slice_in_dim(cot, (1 - core) * width, width, 1)
    cot = jnp.concatenate([kept, lax.ppermute(given, "c", swap)], axis=0)
    tokens, cot = lax.optimization_barrier((tokens, cot))

    def exchange(blocks):
        return lax.all_to_all(blocks, "q", 0, 0)

    def queries_of(second, blocks):
        return call(
            functools.partial(queries_kernel, second),
            "second_queries" if second else "first_queries",
            shape((parts, CORES * share + TAIL * second, width), BF16),
            tokens,
            exchange(blocks).reshape(depth, width),
            cost=(2 * CORES * count * depth * width, 2 * CORES * count * depth),
        )

    def gradient_of(grads):
        grads = lax.all_gather(grads, "near", axis=0, tiled=True)
        grads = lax.all_gather(grads, "far", axis=0, tiled=True)
        summed = lax.dot_general(tokens, grads, (((0,), (0,)), ((), ())), preferred_element_type=F32)
        return exchange(summed.astype(BF16).reshape(groups, CORES * rows, width))

    sent = queries_of(False, spread)
    received = lax.all_to_all(sent, MP, 0, 0)
    outs = (shape((CORES * share, width), F32), shape((CORES * share, width), BF16))
    queries, grads = call(functools.partial(head_kernel, False), "first_heads", outs, received, cot)
    received = gradient_of(grads)

    packed = call(functools.partial(pack_kernel, loss_scale), "pack", blocks, received)
    sent = queries_of(True, packed)
    received = lax.all_to_all(sent, MP, 0, 0)
    squares = call(total_kernel, "total", shape((TAIL, HEAD_DIM), F32), received)
    squares = lax.all_gather(squares, "c", axis=0, tiled=True)
    grads = call(
        functools.partial(head_kernel, True), "second_heads", outs[1], received, squares, queries, cot
    )
    second = call(
        functools.partial(fold_kernel, loss_scale),
        "fold",
        shape((CORES * rows, width), F32),
        gradient_of(grads),
    )
    second = lax.all_gather(second, "c", axis=0, tiled=True)
    whole = shape((rows, columns), F32)
    return call(update_kernel, "update", (whole,) * 3, which, second, weights, moment_one, moment_two)


def solution(mesh):
    groups = mesh.shape["dp"] // CORES
    far = mesh.shape["mp"] // 2
    fine = Mesh(mesh.devices.reshape(groups, CORES, far, 2), ("q", "c") + MP)
    dp = ("q", "c")
    shard = P(MP + dp, None)
    in_specs = (P(dp, MP), P(dp, None), shard, shard, shard)
    return jax.shard_map(local, mesh=fine, in_specs=in_specs, out_specs=(shard,) * 3, check_vma=False)
```

```python
import functools
import math

import jax
import jax.numpy as jnp
from jax import lax
from jax.experimental import pallas as pl
from jax.experimental.pallas import tpu as pltpu
from jax.sharding import Mesh
from jax.sharding import PartitionSpec as P

HEAD_DIM = 128
TAIL = 8
CORES = 2
MP = ("near", "far")
VMEM_BYTES = 16 * 1024 * 1024

radius = 8.0
rate = 0.005
decay_one = 0.9
decay_two = 0.95
weight_decay = 0.1
step_count = 10

BF16 = jnp.bfloat16
F32 = jnp.float32


def pieces_of(value, shape, row):
    high = value.astype(BF16).astype(F32)
    rest = value - high
    middle = rest.astype(BF16).astype(F32)
    low = rest - middle
    rows = lax.broadcasted_iota(jnp.int32, shape, len(shape) - 2)
    lanes = lax.broadcasted_iota(jnp.int32, shape, len(shape) - 1)
    picked = jnp.where(lanes == 0, high, jnp.where(lanes == 1, middle, jnp.where(lanes == 2, low, 0.0)))
    return jnp.where(rows == row, picked, 0.0)


def call(kernel, name, out_shape, *operands, cost=(0, 0)):
    vmem = pl.BlockSpec(memory_space=pltpu.VMEM)
    smem = pl.BlockSpec(memory_space=pltpu.SMEM)
    return pl.pallas_call(
        kernel,
        in_specs=[smem if operand.dtype == jnp.int32 else vmem for operand in operands],
        out_specs=jax.tree.map(lambda _: vmem, out_shape),
        out_shape=out_shape,
        compiler_params=pltpu.CompilerParams(vmem_limit_bytes=VMEM_BYTES),
        cost_estimate=pl.CostEstimate(flops=cost[0], bytes_accessed=cost[1], transcendentals=0),
        name=name,
    )(*operands)


def head_kernel(second, partial_ref, *refs):
    squares_ref, base_ref = refs[:2] if second else (None, None)
    cotangent_ref = refs[2] if second else refs[0]
    out_ref = refs[-1]
    tokens, width = cotangent_ref.shape
    if second:
        squares = squares_ref[0:1, :] + squares_ref[TAIL : TAIL + 1, :]
        scale = radius * lax.rsqrt(squares + 1e-06)
    for head in range(width // HEAD_DIM):
        lanes = slice(head * HEAD_DIM, (head + 1) * HEAD_DIM)
        queries = partial_ref[0, 0:tokens, lanes].astype(F32)
        for part in range(1, partial_ref.shape[0]):
            queries = queries + partial_ref[part, 0:tokens, lanes].astype(F32)
        if second:
            queries = queries * scale + base_ref[:, lanes]
        else:
            refs[-2][:, lanes] = queries
        cotangent = cotangent_ref[:, lanes].astype(F32)
        centred = queries - jnp.mean(queries, axis=-1, keepdims=True)
        spread = jnp.mean(centred * centred, axis=-1, keepdims=True)
        factor = lax.rsqrt(spread + 1e-06)
        normed = centred * factor
        level = jnp.mean(cotangent, axis=-1, keepdims=True)
        along = jnp.mean(cotangent * normed, axis=-1, keepdims=True)
        out_ref[:, lanes] = (factor * (cotangent - level - normed * along)).astype(BF16)


def swapped(core, one, two):
    return jnp.where(core == 0, one, two), jnp.where(core == 0, two, one)


def spread_kernel(core_ref, weights_ref, out_ref):
    width = out_ref.shape[2]
    pair = []
    for side in range(CORES):
        pair.append(swapped(core_ref[0, 0], weights_ref[side, :, :width], weights_ref[side, :, width:])[0])
    block = jnp.concatenate(pair, axis=0).astype(BF16)
    for part in range(out_ref.shape[0]):
        out_ref[part] = block


def pack_kernel(loss_scale, received_ref, out_ref):
    total = received_ref[0].astype(F32)
    for part in range(1, received_ref.shape[0]):
        total = total + received_ref[part].astype(F32)
    block = (total * loss_scale).astype(BF16)
    for part in range(out_ref.shape[0]):
        out_ref[part] = block


def fold_kernel(loss_scale, received_ref, out_ref):
    total = received_ref[0].astype(F32)
    for part in range(1, received_ref.shape[0]):
        total = total + received_ref[part].astype(F32)
    out_ref[...] = total * loss_scale


def update_kernel(core_ref, second_ref, weights_ref, one_ref, two_ref, *out_refs):
    rows = weights_ref.shape[0]
    width = second_ref.shape[1]
    correct_one = 1.0 - decay_one**step_count
    correct_two = 1.0 - decay_two**step_count
    for side in range(CORES):
        start = side * CORES * rows
        lanes = slice(side * width, (side + 1) * width)
        second = swapped(
            core_ref[0, 0],
            second_ref[start : start + rows, :],
            second_ref[start + rows : start + CORES * rows, :],
        )[0]
        weights = weights_ref[:, lanes]
        new_one = decay_one * one_ref[:, lanes] + (1.0 - decay_one) * second
        new_two = decay_two * two_ref[:, lanes] + (1.0 - decay_two) * second * second
        update = new_one / correct_one / (jnp.sqrt(new_two / correct_two) + 1e-08)
        out_refs[0][:, lanes] = weights - rate * (update + weight_decay * weights)
        out_refs[1][:, lanes] = new_one
        out_refs[2][:, lanes] = new_two


def total_kernel(received_ref, out_ref):
    parts, share, _ = received_ref.shape
    block = received_ref[0, share - TAIL : share, 0:HEAD_DIM].astype(F32)
    for part in range(1, parts):
        block = block + received_ref[part, share - TAIL : share, 0:HEAD_DIM].astype(F32)
    out_ref[...] = jnp.full(out_ref.shape, jnp.sum(block), F32)


def queries_kernel(second, tokens_ref, first_ref, out_ref):
    parts, share, width = out_ref.shape
    if second:
        share = share - TAIL
        first = first_ref[...].astype(F32)
        tail = pieces_of(jnp.sum(first * first), (TAIL, width), 0).astype(BF16)
    step = 2
    for group in range(parts // step):
        picked = slice(group * step * share, (group + 1) * step * share)
        value = jnp.dot(tokens_ref[picked, :], first_ref[...], preferred_element_type=F32)
        for part in range(step):
            out_ref[group * step + part, 0:share, :] = value[part * share : (part + 1) * share].astype(BF16)
            if second:
                out_ref[group * step + part, share : share + TAIL, :] = tail


def local(tokens, cotangent, weights, moment_one, moment_two):
    count, depth = tokens.shape
    rows, columns = weights.shape
    groups = lax.axis_size("q")
    parts = lax.axis_size(MP)
    loss_scale = 1.0 / math.sqrt(count * groups * CORES)
    core = lax.axis_index("c")
    share = count // parts
    width = columns // CORES
    shape = jax.ShapeDtypeStruct
    swap = [(0, 1), (1, 0)]

    which = core.reshape(1, 1).astype(jnp.int32)
    blocks = shape((groups, CORES * rows, width), BF16)
    spread = call(spread_kernel, "spread", blocks, which, lax.all_gather(weights, "c", axis=0))
    spread, tokens = lax.optimization_barrier((spread, tokens))

    theirs = lax.ppermute(tokens, "c", swap)
    pair = [side.reshape(parts, share, depth) for side in (tokens, theirs)]
    tokens = jnp.concatenate(pair, axis=1).reshape(-1, depth)

    cot = lax.dynamic_slice_in_dim(cotangent, lax.axis_index(MP) * share, share, 0)
    kept = lax.dynamic_slice_in_dim(cot, core * width, width, 1)
    given = lax.dynamic_slice_in_dim(cot, (1 - core) * width, width, 1)
    cot = jnp.concatenate([kept, lax.ppermute(given, "c", swap)], axis=0)
    tokens, cot = lax.optimization_barrier((tokens, cot))

    def exchange(blocks):
        return lax.all_to_all(blocks, "q", 0, 0)

    def queries_of(second, blocks):
        return call(
            functools.partial(queries_kernel, second),
            "second_queries" if second else "first_queries",
            shape((parts, CORES * share + TAIL * second, width), BF16),
            tokens,
            exchange(blocks).reshape(depth, width),
            cost=(2 * CORES * count * depth * width, 2 * CORES * count * depth),
        )

    def gradient_of(grads):
        grads = lax.all_gather(grads, "far", axis=0, tiled=True)
        grads = lax.all_gather(grads, "near", axis=0, tiled=True)
        summed = lax.dot_general(tokens, grads, (((0,), (0,)), ((), ())), preferred_element_type=F32)
        return exchange(summed.astype(BF16).reshape(groups, CORES * rows, width))

    sent = queries_of(False, spread)
    received = lax.all_to_all(sent, MP, 0, 0)
    outs = (shape((CORES * share, width), F32), shape((CORES * share, width), BF16))
    queries, grads = call(functools.partial(head_kernel, False), "first_heads", outs, received, cot)
    received = gradient_of(grads)

    packed = call(functools.partial(pack_kernel, loss_scale), "pack", blocks, received)
    sent = queries_of(True, packed)
    received = lax.all_to_all(sent, MP, 0, 0)
    squares = call(total_kernel, "total", shape((TAIL, HEAD_DIM), F32), received)
    squares = lax.all_gather(squares, "c", axis=0, tiled=True)
    grads = call(
        functools.partial(head_kernel, True), "second_heads", outs[1], received, squares, queries, cot
    )
    second = call(
        functools.partial(fold_kernel, loss_scale),
        "fold",
        shape((CORES * rows, width), F32),
        gradient_of(grads),
    )
    second = lax.all_gather(second, "c", axis=0, tiled=True)
    whole = shape((rows, columns), F32)
    return call(update_kernel, "update", (whole,) * 3, which, second, weights, moment_one, moment_two)


def solution(mesh):
    groups = mesh.shape["dp"] // CORES
    far = mesh.shape["mp"] // 2
    place = ("far", "near")
    fine = Mesh(mesh.devices.reshape(groups, CORES, far, 2), ("q", "c") + place)
    dp = ("q", "c")
    shard = P(place + dp, None)
    in_specs = (P(dp, place), P(dp, None), shard, shard, shard)
    return jax.shard_map(local, mesh=fine, in_specs=in_specs, out_specs=(shard,) * 3, check_vma=False)
```
